512 devices in a mesh: win: 16 (over y_lo, z), seq: 4 (over y_hi), chan: 8 (over x, core).
Axes of the slice: x: 4, y: 8 (y_hi: 4, y_lo: 2; y = y_hi * 2 + y_lo), z: 8, core: 2. Of those that a mesh axis runs over, the one named last changes fastest.
Arguments:
- first_gate_1: bfloat16 [16, 1024, 4096], P('win', 'seq', 'chan'), may hold values from -6 to 6
- operator_values: bfloat16 [16, 1024, 4096], P('win', 'seq', 'chan'), may hold values from -6 to 6
- second_gate_2: bfloat16 [16, 1024, 4096], P('win', 'seq', 'chan'), may hold values from -6 to 6
- convolved_output: bfloat16 [16, 1024, 4096], P('win', 'seq', 'chan'), may hold values from -6 to 6
- output_gradient: bfloat16 [16, 1024, 4096], P('win', 'seq', 'chan'), may hold values from -6 to 6
- frozen_gradient: bfloat16 [16, 1024, 4096], P('win', 'seq', 'chan'), may hold values from -6 to 6
- filt: bfloat16 [1024, 4096], P('seq', 'chan'), may hold values from -1 to 1
- adapter_down_weight: bfloat16 [4096, 64], P('chan'), may hold values from -0.09375 to 0.09375
- adapter_up_weight: bfloat16 [64, 4096], P(None, 'chan'), may hold values from -0.09375 to 0.09375
Outputs:
- grad_x1: bfloat16 [16, 1024, 4096], P('win', 'seq', 'chan')
- grad_values: bfloat16 [16, 1024, 4096], P('win', 'seq', 'chan')
- grad_x2: bfloat16 [16, 1024, 4096], P('win', 'seq', 'chan')
- grad_a: float32 [4096, 64], P('chan')
- grad_b: float32 [64, 4096], P(None, 'chan')
The draws below stay inside these ranges and needn't reach their ends.
All inputs are finite; a program needn't handle non-finite values.
Results may differ from the reference program's by a relative error of at most 0.005.
Values may be sent and summed in bfloat16 or wider, within the bound.
A program may use at most 64 MiB of HBM per device.

```python
import math
import jax
import jax.numpy as jnp
from jax import lax

MODEL_WIDTH = 4096
ADAPTER_RANK = 64
LEN = 1024
WINDOWS = 16


def draw_filt(key, part):
    key = jax.random.fold_in(key, 7)
    key_rate, key_rough = jax.random.split(key)
    lags = jnp.arange(LEN, dtype=jnp.float32)[:, None]
    spans = jnp.exp(jax.random.uniform(key_rate, (1, MODEL_WIDTH), minval=math.log(30.0), maxval=math.log(8.0 * LEN)))
    envelope = jnp.exp(-lags / spans) / jnp.sqrt(jnp.minimum(spans, 1.0 * LEN))
    rough = jnp.clip(jax.random.normal(key_rough, (LEN, MODEL_WIDTH)), -4.0, 4.0)
    return (envelope * rough).astype(jnp.float32).astype(jnp.bfloat16)


def levels(rng, extent, pieces, smallest, high):
    factor_of, own = 1.0, jax.random.fold_in(rng, 6)
    for dim, blocks in pieces:
        draws = jnp.exp(jax.random.uniform(jax.random.fold_in(own, dim), (blocks,), jnp.float32, smallest / len(pieces), high / len(pieces)))
        factor_of = factor_of * jnp.repeat(draws, extent[dim] // blocks).reshape([-1 if axis == dim else 1 for axis in range(len(extent))])
    return factor_of


def gaussian(stream_key, extent, deviation, limit, cuts=(), kind=jnp.bfloat16):
    drawn = jax.random.normal(stream_key, extent, jnp.float32) * deviation
    if len(cuts) > 0:
        drawn = levels(stream_key, extent, cuts, -0.22, 0.18) * drawn
    return jnp.clip(drawn, min=-limit, max=limit).astype(kind)


def setup_inputs(seed: int = 0) -> dict:
    splits = jax.random.split(jax.random.key(seed), 10)
    return {
        "first_gate_1": gaussian(splits[0], (WINDOWS, LEN, MODEL_WIDTH), 1.0, 6.0, ((0, 16), (1, 4), (2, 8))),
        "operator_values": gaussian(splits[1], (WINDOWS, LEN, MODEL_WIDTH), 1.0, 6.0, ((0, 16), (1, 4), (2, 8))),
        "second_gate_2": gaussian(splits[2], (WINDOWS, LEN, MODEL_WIDTH), 1.0, 6.0, ((0, 16), (1, 4), (2, 8))),
        "convolved_output": gaussian(splits[3], (WINDOWS, LEN, MODEL_WIDTH), 1.0, 6.0, ((0, 16), (1, 4), (2, 8))),
        "output_gradient": gaussian(splits[4], (WINDOWS, LEN, MODEL_WIDTH), 1.0, 6.0, ((0, 16), (1, 4), (2, 8))),
        "frozen_gradient": gaussian(splits[5], (WINDOWS, LEN, MODEL_WIDTH), 1.0, 6.0, ((0, 16), (1, 4), (2, 8))),
        "filt": draw_filt(jax.random.fold_in(splits[9], 71), 0),
        "adapter_down_weight": gaussian(splits[7], (MODEL_WIDTH, ADAPTER_RANK), MODEL_WIDTH ** -0.5, 0.09375, ((0, 8),)),
        "adapter_up_weight": gaussian(splits[8], (ADAPTER_RANK, MODEL_WIDTH), MODEL_WIDTH ** -0.5, 0.09375, ((1, 8),)),
    }


adapter_scaling = 2.0

def reference(first_gate_1, operator_values, second_gate_2, convolved_output, output_gradient, frozen_gradient, filt, adapter_down_weight, adapter_up_weight):
    spec_filter = jnp.conj(jnp.fft.rfft(filt.astype(jnp.float32), n=2 * LEN, axis=0))

    def one_window(items):
        first, values, second, saved, backward_result, frozen_projection = items
        gated_output = (second.astype(jnp.float32) * saved.astype(jnp.float32)).astype(jnp.bfloat16)
        lowrank_input = jnp.dot(gated_output, adapter_down_weight, preferred_element_type=jnp.float32).astype(jnp.bfloat16)
        lowrank_backward = jnp.dot(backward_result, adapter_up_weight.T, preferred_element_type=jnp.float32).astype(jnp.bfloat16)
        gated_gradient = frozen_projection.astype(jnp.float32) + adapter_scaling * jnp.dot(lowrank_backward, adapter_down_weight.T, preferred_element_type=jnp.float32)
        grad_second = (gated_gradient * saved.astype(jnp.float32)).astype(jnp.bfloat16)
        grad_conv = gated_gradient * second.astype(jnp.float32)
        spec_grad = jnp.fft.rfft(grad_conv, n=2 * LEN, axis=0)
        grad_mixed = jnp.fft.irfft(spec_grad * spec_filter, n=2 * LEN, axis=0)[:LEN]
        grad_first = (grad_mixed * values.astype(jnp.float32)).astype(jnp.bfloat16)
        grad_vals = (grad_mixed * first.astype(jnp.float32)).astype(jnp.bfloat16)
        part_a = jnp.dot(gated_output.T, lowrank_backward, preferred_element_type=jnp.float32)
        part_b = jnp.dot(lowrank_input.T, backward_result, preferred_element_type=jnp.float32)
        return (grad_first, grad_vals, grad_second, part_a, part_b)
    grad_x1, grad_values, grad_x2, parts_a, parts_b = lax.map(one_window, (first_gate_1, operator_values, second_gate_2, convolved_output, output_gradient, frozen_gradient))
    factor = adapter_scaling / math.sqrt(WINDOWS * LEN)
    grad_a = factor * lax.optimization_barrier(jnp.sum(parts_a, axis=0))
    grad_b = factor * lax.optimization_barrier(jnp.sum(parts_b, axis=0))
    return (grad_x1, grad_values, grad_x2, grad_a, grad_b)
```

```python
import functools
import math

import jax
import jax.numpy as jnp
import ml_dtypes
import numpy as np
from jax import lax
from jax.experimental import pallas as pl
from jax.experimental.pallas import tpu as pltpu
from jax.sharding import PartitionSpec as P

MESH = pl.DeviceIdType.MESH
bf16 = jnp.bfloat16
f32 = jnp.float32

ROWS = 256
CH = 512
Q = 128
RANK = 64
SEQ = 4
XS = 4
ZS = 8
YS = 8
SL = 2 * RANK // ZS


def fourier_table():
    k = np.arange(ROWS)[:, None]
    t = np.arange(ROWS)[None, :]
    angle = 2.0 * math.pi / (2 * ROWS) * ((2 * k + 1) * t % (4 * ROWS)) / 2.0
    return np.concatenate([np.cos(angle), -np.sin(angle)], axis=0)


def in_two(table):
    high = table.astype(ml_dtypes.bfloat16)
    return high, (table - high.astype(np.float64)).astype(ml_dtypes.bfloat16)


def nt(a, b):
    return lax.dot_general(a, b, (((1,), (1,)), ((), ())), preferred_element_type=f32)


def nn(a, b):
    return lax.dot_general(a, b, (((1,), (0,)), ((), ())), preferred_element_type=f32)


def tn(a, b):
    return lax.dot_general(a, b, (((0,), (0,)), ((), ())), preferred_element_type=f32)


def lanes(i):
    return pl.ds(pl.multiple_of(i * Q, Q), Q)


def kernel(
    factor,
    second_h, conv_h, og_h, frozen_h, filt_h, down_h, up_h, tab_h, itab_h,
    two_h, ab_h,
    second, conv, og, frozen, filt, down, up, tab, itab,
    gm, gx2, ab, gated, pq, pq_in, xs, pqb, fs, gs_send, gs, hs, xf, ys, rs_send, rs,
    ab_send, zr, yr, fin,
    load_sem, core_ss, core_rs, x_ss, x_rs, f_ss, f_rs, g_ss, g_rs, r_ss, r_rs, z_ss, z_rs, y_ss, y_rs, n_ss, n_rs, out_sem,
):
    w = lax.axis_index("win")
    s = lax.axis_index("seq")
    c = lax.axis_index("chan")
    ylo, z = w // ZS, lax.rem(w, ZS)
    y = s * 2 + ylo
    x, core = c // 2, lax.rem(c, 2)

    def at_core():
        return (w, s, x * 2 + 1 - core)

    def at_x(d):
        return (w, s, lax.rem(x + d, XS) * 2 + core)

    def at_seq(d):
        return (w, lax.rem(s + d, SEQ), c)

    def at_z(d):
        return (ylo * ZS + lax.rem(z + d, ZS), s, c)

    def at_y(d):
        other = lax.rem(y + d, YS)
        return (lax.rem(other, 2) * ZS + z, other // 2, c)

    far_x = (2, 1, 3)
    far_seq = (2, 1, 3)
    far_z = (4, 3, 5, 2, 6, 1, 7)
    partners = [at_core()] + [at_x(d) for d in far_x] + [at_z(d) for d in far_z] + [at_y(d) for d in far_z]
    barrier = pltpu.get_barrier_semaphore()
    for p in partners:
        pl.semaphore_signal(barrier, inc=1, device_id=p, device_id_type=MESH)

    loads = {}
    pairs = (
        ("og", og_h, og), ("up", up_h, up), ("second", second_h, second), ("conv", conv_h, conv),
        ("down", down_h, down), ("filt", filt_h, filt), ("frozen", frozen_h, frozen),
        ("tab", tab_h, tab), ("itab", itab_h, itab),
    )
    for i, (name, src, dst) in enumerate(pairs):
        loads[name] = pltpu.make_async_copy(src, dst, load_sem.at[i])
        loads[name].start()

    def remote(src, dst, ss, rs_, dev):
        return pltpu.make_async_remote_copy(
            src_ref=src, dst_ref=dst, send_sem=ss, recv_sem=rs_, device_id=dev, device_id_type=MESH
        )

    def keep(part, base):
        packed = jnp.concatenate([part[: ROWS // 2], part[ROWS // 2 :]], axis=1)
        pq[0, base : base + 64] = packed[:64]
        pq[1, base : base + 64] = packed[64:]

    loads["og"].wait()
    loads["up"].wait()
    keep(nt(og[...], up[...]), 0)
    loads["second"].wait()
    loads["conv"].wait()
    loads["down"].wait()
    gated[...] = (second[...].astype(f32) * conv[...].astype(f32)).astype(bf16)
    keep(nt(gated[...], down[...]), 64)
    loads["filt"].wait()

    pl.semaphore_wait(barrier, len(partners))

    core_a = remote(pq.at[1 - core], pq_in, core_ss.at[0], core_rs.at[0], at_core())
    core_a.start()
    f_copies = []
    for d in far_seq:
        cp = remote(filt.at[:, lanes(lax.rem(s + d, SEQ))], fs.at[s], f_ss.at[d], f_rs.at[d], at_seq(d))
        cp.start()
        f_copies.append(cp)
    core_a.wait_recv()
    xs[x] = pq[core] + pq_in[...]
    x_copies = []
    for d in far_x:
        cp = remote(xs.at[x], xs.at[x], x_ss.at[d], x_rs.at[d], at_x(d))
        cp.start()
        x_copies.append(cp)
    fs[s] = filt[:, lanes(s)]
    for n in ("frozen", "tab", "itab"):
        loads[n].wait()
    for cp in x_copies:
        cp.wait_recv()
    pqb[core] = ((xs[0] + xs[1]) + (xs[2] + xs[3])).astype(bf16)
    core_b = remote(pqb.at[core], pqb.at[core], core_ss.at[1], core_rs.at[1], at_core())
    core_b.start()
    core_b.wait_recv()

    def unpack(base):
        both = jnp.concatenate([pqb[0, base : base + 64], pqb[1, base : base + 64]], axis=0)
        return jnp.concatenate([both[:, :RANK], both[:, RANK:]], axis=0)

    low_back = unpack(0)
    low_in = unpack(64)

    def grad_conv(q):
        gg = frozen[:, lanes(q)].astype(f32) + 2.0 * nn(low_back, down[:, lanes(q)])
        gx2[:, lanes(q)] = (gg * conv[:, lanes(q)].astype(f32)).astype(bf16)
        return (gg * second[:, lanes(q)].astype(f32)).astype(bf16)

    g_copies = []
    for i, d in enumerate(far_seq):
        gs_send[i] = grad_conv(lax.rem(s + d, SEQ))
        cp = remote(gs_send.at[i], gs.at[s], g_ss.at[d], g_rs.at[d], at_seq(d))
        cp.start()
        g_copies.append(cp)

    part_a = tn(low_back, gated[...]).astype(bf16)
    part_b = tn(low_in, og[...]).astype(bf16)
    for i in range(ZS // 2):
        ab_send[i] = part_a[SL * i : SL * (i + 1)]
        ab_send[ZS // 2 + i] = part_b[SL * i : SL * (i + 1)]
    z_copies = []
    for d in far_z:
        cp = remote(ab_send.at[lax.rem(z + d, ZS)], zr.at[z], z_ss.at[d], z_rs.at[d], at_z(d))
        cp.start()
        z_copies.append(cp)
    zr[z] = ab_send[z]
    gs[s] = grad_conv(s)
    out_copies = [pltpu.make_async_copy(gx2, two_h.at[pl.ds(ROWS, ROWS)], out_sem.at[0])]
    out_copies[0].start()

    def transform(block):
        both = nn(tab[...], block)
        return both[: 2 * ROWS] + both[2 * ROWS :]

    for cp in f_copies:
        cp.wait_recv()
    sign = (1 - 2 * lax.rem(lax.broadcasted_iota(jnp.int32, (ROWS, Q), 0), 2)).astype(f32)
    before = None
    for lag in range(SEQ):
        spec = transform(fs[lag])
        re, im = spec[:ROWS], spec[ROWS:]
        if before is None:
            hs[lag, :ROWS] = re
            hs[lag, ROWS:] = im
        else:
            hs[lag, :ROWS] = re - sign * before[1]
            hs[lag, ROWS:] = im + sign * before[0]
        before = (re, im)

    for cp in z_copies:
        cp.wait_recv()
    total = zr[0].astype(f32)
    for i in range(1, ZS):
        total = total + zr[i].astype(f32)
    yr[y] = total.astype(bf16)
    y_copies = []
    for d in far_z:
        cp = remote(yr.at[y], yr.at[y], y_ss.at[d], y_rs.at[d], at_y(d))
        cp.start()
        y_copies.append(cp)

    for cp in g_copies:
        cp.wait_recv()
    for i in range(SEQ):
        xf[i] = transform(gs[i])
    for j in range(SEQ - 1, -1, -1):
        for r in range(0, ROWS, 64):
            yre = jnp.zeros((64, Q), f32)
            yim = jnp.zeros((64, Q), f32)
            for i in range(j, SEQ):
                a, b = xf[i, r : r + 64], xf[i, ROWS + r : ROWS + r + 64]
                p, q = hs[i - j, r : r + 64], hs[i - j, ROWS + r : ROWS + r + 64]
                yre = yre + a * p + b * q
                yim = yim + b * p - a * q
            ys[r : r + 64] = yre.astype(bf16)
            ys[ROWS + r : ROWS + r + 64] = yim.astype(bf16)
        spec = ys[...]
        out = (nn(itab[...], jnp.concatenate([spec, spec], axis=0)) * (1.0 / ROWS)).astype(bf16)
        rs_send[j] = out

        @pl.when(s != j)
        def _():
            d = lax.rem(j - s + SEQ, SEQ)
            remote(rs_send.at[j], rs.at[s], r_ss.at[d], r_rs.at[d], (w, j, c)).start()

    gm[:, lanes(s)] = rs_send[s]

    for cp in y_copies:
        cp.wait_recv()
    total = yr[0].astype(f32)
    for i in range(1, YS):
        total = total + yr[i].astype(f32)
    fin[z] = (total * factor).astype(bf16)
    n_copies = []
    for d in far_z:
        cp = remote(fin.at[z], fin.at[z], n_ss.at[d], n_rs.at[d], at_z(d))
        cp.start()
        n_copies.append(cp)

    r_copies = []
    for d in (1, 3, 2):
        other = lax.rem(s + d, SEQ)
        cp = remote(rs_send.at[other], rs.at[s], r_ss.at[d], r_rs.at[d], at_seq(d))
        r_copies.append(cp)
    for d, cp in zip((1, 3, 2), r_copies, strict=True):
        cp.wait_recv()
        source = lax.rem(s - d + SEQ, SEQ)
        gm[:, lanes(source)] = rs[source]
    out_copies.append(pltpu.make_async_copy(gm, two_h.at[pl.ds(0, ROWS)], out_sem.at[1]))
    out_copies[1].start()
    for cp in n_copies:
        cp.wait_recv()
    for i in range(ZS):
        ab[SL * i : SL * (i + 1)] = fin[i].astype(f32)

    out_copies.append(pltpu.make_async_copy(ab, ab_h, out_sem.at[2]))
    out_copies[2].start()
    for cp in [core_a, core_b] + f_copies + x_copies + g_copies + z_copies + y_copies + r_copies + n_copies:
        cp.wait_send()
    for cp in out_copies:
        cp.wait()


def on_device(
    first_gate_1, operator_values, second_gate_2, convolved_output, output_gradient,
    frozen_gradient, filt, adapter_down_weight, adapter_up_weight,
):
    positions = lax.axis_size("win") * first_gate_1.shape[0] * first_gate_1.shape[1] * lax.axis_size("seq")
    factor = 2.0 / math.sqrt(positions)
    table = fourier_table()
    tab = jnp.asarray(np.concatenate(in_two(table), axis=0))
    itab = jnp.asarray(np.concatenate(in_two(np.ascontiguousarray(table.T)), axis=1))
    blk = functools.partial(pltpu.VMEM, (ROWS, CH))
    dma = pltpu.SemaphoreType.DMA
    two, ab = pl.pallas_call(
        functools.partial(kernel, factor),
        out_shape=(
            jax.ShapeDtypeStruct((2 * ROWS, CH), bf16),
            jax.ShapeDtypeStruct((2 * RANK, CH), f32),
        ),
        in_specs=[pl.BlockSpec(memory_space=pltpu.HBM)] * 9,
        out_specs=tuple([pl.BlockSpec(memory_space=pltpu.HBM)] * 2),
        scratch_shapes=[
            blk(bf16), blk(bf16), blk(bf16), blk(bf16), blk(bf16),
            pltpu.VMEM((RANK, CH), bf16), pltpu.VMEM((RANK, CH), bf16),
            pltpu.VMEM((4 * ROWS, ROWS), bf16), pltpu.VMEM((ROWS, 4 * ROWS), bf16),
            blk(bf16), blk(bf16), pltpu.VMEM((2 * RANK, CH), f32),
            blk(bf16),
            pltpu.VMEM((2, 128, 128), f32), pltpu.VMEM((128, 128), f32),
            pltpu.VMEM((XS, 128, 128), f32), pltpu.VMEM((2, 128, 128), bf16),
            pltpu.VMEM((SEQ, ROWS, Q), bf16),
            pltpu.VMEM((SEQ - 1, ROWS, Q), bf16), pltpu.VMEM((SEQ, ROWS, Q), bf16),
            pltpu.VMEM((SEQ, 2 * ROWS, Q), f32), pltpu.VMEM((SEQ, 2 * ROWS, Q), f32),
            pltpu.VMEM((2 * ROWS, Q), bf16),
            pltpu.VMEM((SEQ, ROWS, Q), bf16), pltpu.VMEM((SEQ, ROWS, Q), bf16),
            pltpu.VMEM((ZS, SL, CH), bf16), pltpu.VMEM((ZS, SL, CH), bf16),
            pltpu.VMEM((YS, SL, CH), bf16), pltpu.VMEM((ZS, SL, CH), bf16),
            dma((9,)), dma((2,)), dma((2,)), dma((XS,)), dma((XS,)),
            dma((SEQ,)), dma((SEQ,)), dma((SEQ,)), dma((SEQ,)), dma((SEQ,)), dma((SEQ,)),
            dma((ZS,)), dma((ZS,)), dma((YS,)), dma((YS,)), dma((ZS,)), dma((ZS,)), dma((3,)),
        ],
        compiler_params=pltpu.CompilerParams(
            collective_id=0, has_side_effects=True, vmem_limit_bytes=60 * 1024 * 1024
        ),
        name="window_backward",
    )(
        second_gate_2[0], convolved_output[0], output_gradient[0], frozen_gradient[0], filt,
        adapter_down_weight.T, adapter_up_weight, tab, itab,
    )
    gm = two[:ROWS].astype(f32)
    grad_x1 = (gm * operator_values[0].astype(f32)).astype(bf16)
    grad_values = (gm * first_gate_1[0].astype(f32)).astype(bf16)
    return grad_x1[None], grad_values[None], two[ROWS:][None], ab[:RANK].T, ab[RANK:]


def solution(mesh):
    block = P("win", "seq", "chan")
    in_specs = (block,) * 6 + (P("seq", "chan"), P("chan", None), P(None, "chan"))
    out_specs = (block,) * 3 + (P("chan", None), P(None, "chan"))
    return jax.shard_map(
        on_device, mesh=mesh, in_specs=in_specs, out_specs=out_specs, check_vma=False
    )
```

```python
import functools
import math

import jax
import jax.numpy as jnp
import ml_dtypes
import numpy as np
from jax import lax
from jax.experimental import pallas as pl
from jax.experimental.pallas import tpu as pltpu
from jax.sharding import PartitionSpec as P

MESH = pl.DeviceIdType.MESH
bf16 = jnp.bfloat16
f32 = jnp.float32

ROWS = 256
CH = 512
Q = 128
RANK = 64
SEQ = 4
XS = 4
ZS = 8
YS = 8
SL = 2 * RANK // ZS


def fourier_table():
    k = np.arange(ROWS)[:, None]
    t = np.arange(ROWS)[None, :]
    angle = 2.0 * math.pi / (2 * ROWS) * ((2 * k + 1) * t % (4 * ROWS)) / 2.0
    return np.concatenate([np.cos(angle), -np.sin(angle)], axis=0)


def in_two(table):
    high = table.astype(ml_dtypes.bfloat16)
    return high, (table - high.astype(np.float64)).astype(ml_dtypes.bfloat16)


def nt(a, b):
    return lax.dot_general(a, b, (((1,), (1,)), ((), ())), preferred_element_type=f32)


def nn(a, b):
    return lax.dot_general(a, b, (((1,), (0,)), ((), ())), preferred_element_type=f32)


def tn(a, b):
    return lax.dot_general(a, b, (((0,), (0,)), ((), ())), preferred_element_type=f32)


def lanes(i):
    return pl.ds(pl.multiple_of(i * Q, Q), Q)


def kernel(
    factor,
    second_h, conv_h, og_h, frozen_h, filt_h, down_h, up_h, tab_h, itab_h,
    gm_h, gx2_h, fin_h,
    second, conv, og, frozen, filt, down, up, tab, itab,
    gx2, gated, pq, pq_in, xs, pqb, fs, gs_send, gs, hs, xf, ys, rs_send,
    ab_send, zr, yr, fin,
    load_sem, core_ss, core_rs, x_ss, x_rs, f_ss, f_rs, g_ss, g_rs, r_ss, r_rs, z_ss, z_rs, y_ss, y_rs, n_ss, n_rs, out_sem,
):
    w = lax.axis_index("win")
    s = lax.axis_index("seq")
    c = lax.axis_index("chan")
    ylo, z = w // ZS, lax.rem(w, ZS)
    y = s * 2 + ylo
    x, core = c // 2, lax.rem(c, 2)

    def at_core():
        return (w, s, x * 2 + 1 - core)

    def at_x(d):
        return (w, s, lax.rem(x + d, XS) * 2 + core)

    def at_seq(d):
        return (w, lax.rem(s + d, SEQ), c)

    def at_z(d):
        return (ylo * ZS + lax.rem(z + d, ZS), s, c)

    def at_y(d):
        other = lax.rem(y + d, YS)
        return (lax.rem(other, 2) * ZS + z, other // 2, c)

    far_x = (2, 1, 3)
    far_seq = (2, 1, 3)
    far_z = (4, 3, 5, 2, 6, 1, 7)
    partners = [at_core()] + [at_x(d) for d in far_x] + [at_z(d) for d in far_z] + [at_y(d) for d in far_z]
    barrier = pltpu.get_barrier_semaphore()
    for p in partners:
        pl.semaphore_signal(barrier, inc=1, device_id=p, device_id_type=MESH)

    loads = {}
    pairs = (
        ("og", og_h, og), ("up", up_h, up), ("second", second_h, second), ("conv", conv_h, conv),
        ("down", down_h, down), ("filt", filt_h, filt), ("frozen", frozen_h, frozen),
        ("tab", tab_h, tab), ("itab", itab_h, itab),
    )
    for i, (name, src, dst) in enumerate(pairs):
        loads[name] = pltpu.make_async_copy(src, dst, load_sem.at[i])
        loads[name].start()

    def remote(src, dst, ss, rs_, dev):
        return pltpu.make_async_remote_copy(
            src_ref=src, dst_ref=dst, send_sem=ss, recv_sem=rs_, device_id=dev, device_id_type=MESH
        )

    def keep(part, base):
        packed = jnp.concatenate([part[: ROWS // 2], part[ROWS // 2 :]], axis=1)
        pq[0, base : base + 64] = packed[:64]
        pq[1, base : base + 64] = packed[64:]

    loads["og"].wait()
    loads["up"].wait()
    keep(nt(og[...], up[...]), 0)
    loads["second"].wait()
    loads["conv"].wait()
    loads["down"].wait()
    gated[...] = (second[...].astype(f32) * conv[...].astype(f32)).astype(bf16)
    keep(nt(gated[...], down[...]), 64)
    loads["filt"].wait()

    pl.semaphore_wait(barrier, len(partners))

    core_a = remote(pq.at[1 - core], pq_in, core_ss.at[0], core_rs.at[0], at_core())
    core_a.start()
    f_copies = []
    for d in far_seq:
        cp = remote(filt.at[:, lanes(lax.rem(s + d, SEQ))], fs.at[s], f_ss.at[d], f_rs.at[d], at_seq(d))
        cp.start()
        f_copies.append(cp)
    core_a.wait_recv()
    xs[x] = (pq[core] + pq_in[...]).astype(bf16)
    x_copies = []
    for d in far_x:
        cp = remote(xs.at[x], xs.at[x], x_ss.at[d], x_rs.at[d], at_x(d))
        cp.start()
        x_copies.append(cp)
    fs[s] = filt[:, lanes(s)]
    for n in ("frozen", "tab", "itab"):
        loads[n].wait()
    for cp in x_copies:
        cp.wait_recv()
    parts = [xs[i].astype(f32) for i in range(XS)]
    pqb[core] = ((parts[0] + parts[1]) + (parts[2] + parts[3])).astype(bf16)
    core_b = remote(pqb.at[core], pqb.at[core], core_ss.at[1], core_rs.at[1], at_core())
    core_b.start()
    core_b.wait_recv()

    def unpack(base):
        both = jnp.concatenate([pqb[0, base : base + 64], pqb[1, base : base + 64]], axis=0)
        return jnp.concatenate([both[:, :RANK], both[:, RANK:]], axis=0)

    low_back = unpack(0)
    low_in = unpack(64)

    def grad_conv(q):
        gg = frozen[:, lanes(q)].astype(f32) + 2.0 * nn(low_back, down[:, lanes(q)])
        gx2[:, lanes(q)] = (gg * conv[:, lanes(q)].astype(f32)).astype(bf16)
        return (gg * second[:, lanes(q)].astype(f32)).astype(bf16)

    part_a = tn(low_back, gated[...]).astype(bf16)
    part_b = tn(low_in, og[...]).astype(bf16)
    for i in range(ZS // 2):
        ab_send[i] = part_a[SL * i : SL * (i + 1)]
        ab_send[ZS // 2 + i] = part_b[SL * i : SL * (i + 1)]
    z_copies = []
    for d in far_z:
        cp = remote(ab_send.at[lax.rem(z + d, ZS)], zr.at[z], z_ss.at[d], z_rs.at[d], at_z(d))
        cp.start()
        z_copies.append(cp)
    zr[z] = ab_send[z]
    g_copies = []
    for i, d in enumerate(far_seq):
        gs_send[i] = grad_conv(lax.rem(s + d, SEQ))
        cp = remote(gs_send.at[i], gs.at[s], g_ss.at[d], g_rs.at[d], at_seq(d))
        cp.start()
        g_copies.append(cp)

    gs[s] = grad_conv(s)
    out_copies = [pltpu.make_async_copy(gx2, gx2_h, out_sem.at[0])]
    out_copies[0].start()

    def transform(src, dst, i, j):
        both = jnp.concatenate([src[i], src[j]], axis=1)
        spec = nn(tab[...], jnp.concatenate([both, both], axis=0))
        dst[i] = spec[:, :Q]
        dst[j] = spec[:, Q:]

    for cp in f_copies:
        cp.wait_recv()

    @pl.loop(0, SEQ // 2)
    def _(i):
        transform(fs, hs, 2 * i, 2 * i + 1)

    sign = (1 - 2 * lax.rem(lax.broadcasted_iota(jnp.int32, (64, Q), 0), 2)).astype(f32)

    @pl.loop(0, ROWS // 64)
    def _(r):
        up_rows = pl.ds(pl.multiple_of(r * 64, 64), 64)
        low_rows = pl.ds(pl.multiple_of(ROWS + r * 64, 64), 64)
        spec = [(hs[lag, up_rows], hs[lag, low_rows]) for lag in range(SEQ)]
        for lag in range(1, SEQ):
            hs[lag, up_rows] = spec[lag][0] - sign * spec[lag - 1][1]
            hs[lag, low_rows] = spec[lag][1] + sign * spec[lag - 1][0]

    for cp in z_copies:
        cp.wait_recv()
    total = zr[0].astype(f32)
    for i in range(1, ZS):
        total = total + zr[i].astype(f32)
    yr[y] = total.astype(bf16)
    y_copies = []
    for d in far_z:
        cp = remote(yr.at[y], yr.at[y], y_ss.at[d], y_rs.at[d], at_y(d))
        cp.start()
        y_copies.append(cp)

    g_by = dict(zip(far_seq, g_copies, strict=True))

    def from_seq(d):
        return lax.rem(s - d + SEQ, SEQ)

    g_by[1].wait_recv()
    transform(gs, xf, s, from_seq(1))
    g_by[3].wait_recv()
    g_by[2].wait_recv()
    transform(gs, xf, from_seq(3), from_seq(2))
    r_copies = []
    for pair in ((2, 1), (3, 0)):
        blocks = [lax.rem(s + d, SEQ) for d in pair]

        @pl.loop(0, ROWS // 64)
        def _(r):
            up_rows = pl.ds(pl.multiple_of(r * 64, 64), 64)
            low_rows = pl.ds(pl.multiple_of(ROWS + r * 64, 64), 64)
            for side, j in enumerate(blocks):

                def add(i, sums):
                    a, b = xf[i, up_rows], xf[i, low_rows]
                    p, q = hs[i - j, up_rows], hs[i - j, low_rows]
                    return sums[0] + a * p + b * q, sums[1] + b * p - a * q

                zeros = jnp.zeros((64, Q), f32)
                yre, yim = lax.fori_loop(j, SEQ, add, (zeros, zeros))
                ys[up_rows, side * Q : side * Q + Q] = yre.astype(bf16)
                ys[low_rows, side * Q : side * Q + Q] = yim.astype(bf16)

        spec = ys[...]
        out = (nn(itab[...], jnp.concatenate([spec, spec], axis=0)) * (1.0 / ROWS)).astype(bf16)
        for side, d in enumerate(pair):
            rs_send[d] = out[:, side * Q : side * Q + Q]
            if d:
                cp = remote(rs_send.at[d], gm_h.at[s], r_ss.at[d], r_rs.at[d], at_seq(d))
                r_copies.append(cp)
            else:
                cp = pltpu.make_async_copy(rs_send.at[d], gm_h.at[s], out_sem.at[1])
                out_copies.append(cp)
            cp.start()

    for cp in y_copies:
        cp.wait_recv()
    total = yr[0].astype(f32)
    for i in range(1, YS):
        total = total + yr[i].astype(f32)
    fin[...] = (total * factor).astype(bf16)
    n_copies = []
    for d in far_z:
        cp = remote(fin, fin_h.at[z], n_ss.at[d], n_rs.at[d], at_z(d))
        cp.start()
        n_copies.append(cp)

    out_copies.append(pltpu.make_async_copy(fin, fin_h.at[z], out_sem.at[2]))
    out_copies[-1].start()

    for cp in r_copies + n_copies:
        cp.wait_recv()
    for cp in [core_a, core_b] + f_copies + x_copies + g_copies + z_copies + y_copies + r_copies + n_copies:
        cp.wait_send()
    for cp in out_copies:
        cp.wait()


def results_kernel(
    gm_h, gx2_h, fin_h, values_h, first_h, x1_h, val_h, x2_h, a_h, b_h,
    gm, values, first, x1, val, x2, fin, low, in_sem, out_sem,
):
    halves = [pl.ds(0, ROWS // 2), pl.ds(ROWS // 2, ROWS // 2)]
    loads = []
    stores = []

    def fetch(src, dst):
        loads.append(pltpu.make_async_copy(src, dst, in_sem.at[len(loads)]))
        loads[-1].start()

    def put(src, dst):
        stores.append(pltpu.make_async_copy(src, dst, out_sem.at[len(stores)]))
        stores[-1].start()

    for rows in halves:
        fetch(gm_h.at[:, rows], gm.at[:, rows])
        fetch(values_h.at[rows], values.at[rows])
        fetch(first_h.at[rows], first.at[rows])
    fetch(gx2_h, x2)
    fetch(fin_h, fin)
    for i, rows in enumerate(halves):
        for cp in loads[3 * i : 3 * i + 3]:
            cp.wait()
        for q in range(SEQ):
            cols = slice(q * Q, q * Q + Q)
            mixed = gm[q, rows].astype(f32)
            x1[rows, cols] = (mixed * values[rows, cols].astype(f32)).astype(bf16)
            val[rows, cols] = (mixed * first[rows, cols].astype(f32)).astype(bf16)
        put(x1.at[rows], x1_h.at[rows])
        put(val.at[rows], val_h.at[rows])
    for cp in loads[6:]:
        cp.wait()
    put(x2, x2_h)
    for i in range(ZS):
        low[SL * i : SL * (i + 1)] = fin[i].astype(f32)
    put(low.at[pl.ds(0, RANK)], a_h)
    put(low.at[pl.ds(RANK, RANK)], b_h)
    for cp in stores:
        cp.wait()


def on_device(
    first_gate_1, operator_values, second_gate_2, convolved_output, output_gradient,
    frozen_gradient, filt, adapter_down_weight, adapter_up_weight,
):
    positions = lax.axis_size("win") * first_gate_1.shape[0] * first_gate_1.shape[1] * lax.axis_size("seq")
    factor = 2.0 / math.sqrt(positions)
    table = fourier_table()
    tab = jnp.asarray(np.concatenate(in_two(table), axis=1))
    itab = jnp.asarray(np.concatenate(in_two(np.ascontiguousarray(table.T)), axis=1))
    blk = functools.partial(pltpu.VMEM, (ROWS, CH))
    dma = pltpu.SemaphoreType.DMA
    mixed, grad_x2, slices = pl.pallas_call(
        functools.partial(kernel, factor),
        out_shape=(
            jax.ShapeDtypeStruct((SEQ, ROWS, Q), bf16),
            jax.ShapeDtypeStruct((ROWS, CH), bf16),
            jax.ShapeDtypeStruct((ZS, SL, CH), bf16),
        ),
        in_specs=[pl.BlockSpec(memory_space=pltpu.HBM)] * 9,
        out_specs=tuple([pl.BlockSpec(memory_space=pltpu.HBM)] * 3),
        scratch_shapes=[
            blk(bf16), blk(bf16), blk(bf16), blk(bf16), blk(bf16),
            pltpu.VMEM((RANK, CH), bf16), pltpu.VMEM((RANK, CH), bf16),
            pltpu.VMEM((2 * ROWS, 2 * ROWS), bf16), pltpu.VMEM((ROWS, 4 * ROWS), bf16),
            blk(bf16),
            blk(bf16),
            pltpu.VMEM((2, 128, 128), f32), pltpu.VMEM((128, 128), f32),
            pltpu.VMEM((XS, 128, 128), bf16), pltpu.VMEM((2, 128, 128), bf16),
            pltpu.VMEM((SEQ, ROWS, Q), bf16),
            pltpu.VMEM((SEQ - 1, ROWS, Q), bf16), pltpu.VMEM((SEQ, ROWS, Q), bf16),
            pltpu.VMEM((SEQ, 2 * ROWS, Q), f32), pltpu.VMEM((SEQ, 2 * ROWS, Q), f32),
            pltpu.VMEM((2 * ROWS, 2 * Q), bf16),
            pltpu.VMEM((SEQ, ROWS, Q), bf16),
            pltpu.VMEM((ZS, SL, CH), bf16), pltpu.VMEM((ZS, SL, CH), bf16),
            pltpu.VMEM((YS, SL, CH), bf16), pltpu.VMEM((SL, CH), bf16),
            dma((9,)), dma((2,)), dma((2,)), dma((XS,)), dma((XS,)),
            dma((SEQ,)), dma((SEQ,)), dma((SEQ,)), dma((SEQ,)), dma((SEQ,)), dma((SEQ,)),
            dma((ZS,)), dma((ZS,)), dma((YS,)), dma((YS,)), dma((ZS,)), dma((ZS,)), dma((3,)),
        ],
        compiler_params=pltpu.CompilerParams(
            collective_id=0, has_side_effects=True, vmem_limit_bytes=60 * 1024 * 1024
        ),
        name="window_backward",
    )(
        second_gate_2[0], convolved_output[0], output_gradient[0], frozen_gradient[0], filt,
        adapter_down_weight.T, adapter_up_weight, tab, itab,
    )
    wide = jax.ShapeDtypeStruct((ROWS, CH), bf16)
    low = jax.ShapeDtypeStruct((RANK, CH), f32)
    grad_x1, grad_values, grad_x2, grad_a, grad_b = pl.pallas_call(
        results_kernel,
        out_shape=(wide, wide, wide, low, low),
        in_specs=[pl.BlockSpec(memory_space=pl.ANY)] * 5,
        out_specs=tuple([pl.BlockSpec(memory_space=pl.ANY)] * 5),
        scratch_shapes=[pltpu.VMEM((SEQ, ROWS, Q), bf16)] + [blk(bf16)] * 5
        + [pltpu.VMEM((ZS, SL, CH), bf16), pltpu.VMEM((2 * RANK, CH), f32), dma((8,)), dma((7,))],
        compiler_params=pltpu.CompilerParams(vmem_limit_bytes=60 * 1024 * 1024),
        name="results",
    )(mixed, grad_x2, slices, operator_values[0], first_gate_1[0])
    return grad_x1[None], grad_values[None], grad_x2[None], grad_a.T, grad_b


def solution(mesh):
    block = P("win", "seq", "chan")
    in_specs = (block,) * 6 + (P("seq", "chan"), P("chan", None), P(None, "chan"))
    out_specs = (block,) * 3 + (P("chan", None), P(None, "chan"))
    return jax.shard_map(
        on_device, mesh=mesh, in_specs=in_specs, out_specs=out_specs, check_vma=False
    )
```

```python
import functools
import math

import jax
import jax.numpy as jnp
import ml_dtypes
import numpy as np
from jax import lax
from jax.experimental import pallas as pl
from jax.experimental.pallas import tpu as pltpu
from jax.sharding import PartitionSpec as P

MESH = pl.DeviceIdType.MESH
bf16 = jnp.bfloat16
f32 = jnp.float32

ROWS = 256
CH = 512
Q = 128
RANK = 64
SEQ = 4
XS = 4
ZS = 8
YS = 8
SL = 2 * RANK // ZS


def fourier_table():
    k = np.arange(ROWS)[:, None]
    t = np.arange(ROWS)[None, :]
    angle = 2.0 * math.pi / (2 * ROWS) * ((2 * k + 1) * t % (4 * ROWS)) / 2.0
    return np.concatenate([np.cos(angle), -np.sin(angle)], axis=0)


def in_two(table):
    high = table.astype(ml_dtypes.bfloat16)
    return high, (table - high.astype(np.float64)).astype(ml_dtypes.bfloat16)


def nt(a, b):
    return lax.dot_general(a, b, (((1,), (1,)), ((), ())), preferred_element_type=f32)


def nn(a, b):
    return lax.dot_general(a, b, (((1,), (0,)), ((), ())), preferred_element_type=f32)


def tn(a, b):
    return lax.dot_general(a, b, (((0,), (0,)), ((), ())), preferred_element_type=f32)


def lanes(i):
    return pl.ds(pl.multiple_of(i * Q, Q), Q)


def kernel(
    factor,
    second_h, conv_h, og_h, frozen_h, filt_h, down_h, up_h, tab_h, itab_h,
    gm_h, gx2_h, fin_h,
    second, conv, og, frozen, filt, down, up, tab, itab,
    gx2, gated, pq, pq_in, xs, pqb, fs, gs_send, gs, hs, xf, ys, rs_send,
    ab_send, zr, yr, fin,
    load_sem, core_ss, core_rs, x_ss, x_rs, f_ss, f_rs, g_ss, g_rs, r_ss, r_rs, z_ss, z_rs, y_ss, y_rs, n_ss, n_rs, out_sem, answer_sem,
):
    w = lax.axis_index("win")
    s = lax.axis_index("seq")
    c = lax.axis_index("chan")
    ylo, z = w // ZS, lax.rem(w, ZS)
    y = s * 2 + ylo
    x, core = c // 2, lax.rem(c, 2)

    def at_core():
        return (w, s, x * 2 + 1 - core)

    def at_x(d):
        return (w, s, lax.rem(x + d, XS) * 2 + core)

    def at_seq(d):
        return (w, lax.rem(s + d, SEQ), c)

    def at_z(d):
        return (ylo * ZS + lax.rem(z + d, ZS), s, c)

    def at_y(d):
        other = lax.rem(y + d, YS)
        return (lax.rem(other, 2) * ZS + z, other // 2, c)

    far_x = (2, 1, 3)
    far_seq = (2, 1, 3)
    far_z = (4, 3, 5, 2, 6, 1, 7)
    partners = [at_core()] + [at_x(d) for d in far_x] + [at_y(d) for d in far_z]
    barrier = pltpu.get_barrier_semaphore()

    def greet(semaphore, wanted):
        for d in far_z:
            @pl.when(wanted(lax.rem(z + d, ZS)))
            def _():
                pl.semaphore_signal(semaphore, inc=1, device_id=at_z(d), device_id_type=MESH)

    greet(barrier, lambda other: other > z)
    for p in partners:
        pl.semaphore_signal(barrier, inc=1, device_id=p, device_id_type=MESH)

    loads = {}
    pairs = (
        ("og", og_h, og), ("up", up_h, up), ("second", second_h, second), ("conv", conv_h, conv),
        ("down", down_h, down), ("filt", filt_h, filt), ("frozen", frozen_h, frozen),
        ("tab", tab_h, tab), ("itab", itab_h, itab),
    )
    for i, (name, src, dst) in enumerate(pairs):
        loads[name] = pltpu.make_async_copy(src, dst, load_sem.at[i])
        loads[name].start()

    def remote(src, dst, ss, rs_, dev):
        return pltpu.make_async_remote_copy(
            src_ref=src, dst_ref=dst, send_sem=ss, recv_sem=rs_, device_id=dev, device_id_type=MESH
        )

    def keep(part, base):
        packed = jnp.concatenate([part[: ROWS // 2], part[ROWS // 2 :]], axis=1)
        pq[0, base : base + 64] = packed[:64]
        pq[1, base : base + 64] = packed[64:]

    loads["og"].wait()
    loads["up"].wait()
    keep(nt(og[...], up[...]), 0)
    loads["second"].wait()
    loads["conv"].wait()
    loads["down"].wait()
    gated[...] = (second[...].astype(f32) * conv[...].astype(f32)).astype(bf16)
    keep(nt(gated[...], down[...]), 64)
    loads["filt"].wait()

    pl.semaphore_wait(barrier, len(partners) + z)
    greet(answer_sem, lambda other: other < z)

    core_a = remote(pq.at[1 - core], pq_in, core_ss.at[0], core_rs.at[0], at_core())
    core_a.start()
    f_copies = []
    for d in far_seq:
        cp = remote(filt.at[:, lanes(lax.rem(s + d, SEQ))], fs.at[s], f_ss.at[d], f_rs.at[d], at_seq(d))
        cp.start()
        f_copies.append(cp)
    core_a.wait_recv()
    xs[x] = (pq[core] + pq_in[...]).astype(bf16)
    x_copies = []
    for d in far_x:
        cp = remote(xs.at[x], xs.at[x], x_ss.at[d], x_rs.at[d], at_x(d))
        cp.start()
        x_copies.append(cp)
    fs[s] = filt[:, lanes(s)]
    for n in ("frozen", "tab", "itab"):
        loads[n].wait()
    for cp in x_copies:
        cp.wait_recv()
    parts = [xs[i].astype(f32) for i in range(XS)]
    pqb[core] = ((parts[0] + parts[1]) + (parts[2] + parts[3])).astype(bf16)
    core_b = remote(pqb.at[core], pqb.at[core], core_ss.at[1], core_rs.at[1], at_core())
    core_b.start()
    core_b.wait_recv()

    def unpack(base):
        both = jnp.concatenate([pqb[0, base : base + 64], pqb[1, base : base + 64]], axis=0)
        return jnp.concatenate([both[:, :RANK], both[:, RANK:]], axis=0)

    low_back = unpack(0)
    low_in = unpack(64)

    def grad_conv(q):
        gg = frozen[:, lanes(q)].astype(f32) + 2.0 * nn(low_back, down[:, lanes(q)])
        gx2[:, lanes(q)] = (gg * conv[:, lanes(q)].astype(f32)).astype(bf16)
        return (gg * second[:, lanes(q)].astype(f32)).astype(bf16)

    part_a = tn(low_back, gated[...]).astype(bf16)
    part_b = tn(low_in, og[...]).astype(bf16)
    for i in range(ZS // 2):
        ab_send[i] = part_a[SL * i : SL * (i + 1)]
        ab_send[ZS // 2 + i] = part_b[SL * i : SL * (i + 1)]

    @pl.when(z < ZS - 1)
    def _():
        pl.semaphore_wait(answer_sem, ZS - 1 - z)

    z_copies = []
    for d in far_z:
        cp = remote(ab_send.at[lax.rem(z + d, ZS)], zr.at[z], z_ss.at[d], z_rs.at[d], at_z(d))
        cp.start()
        z_copies.append(cp)
    zr[z] = ab_send[z]
    g_copies = []
    for i, d in enumerate(far_seq):
        gs_send[i] = grad_conv(lax.rem(s + d, SEQ))
        cp = remote(gs_send.at[i], gs.at[s], g_ss.at[d], g_rs.at[d], at_seq(d))
        cp.start()
        g_copies.append(cp)

    gs[s] = grad_conv(s)
    out_copies = [pltpu.make_async_copy(gx2, gx2_h, out_sem.at[0])]
    out_copies[0].start()

    def transform(src, dst, i, j):
        both = jnp.concatenate([src[i], src[j]], axis=1)
        spec = nn(tab[...], jnp.concatenate([both, both], axis=0))
        dst[i] = spec[:, :Q]
        dst[j] = spec[:, Q:]

    for cp in f_copies:
        cp.wait_recv()

    @pl.loop(0, SEQ // 2)
    def _(i):
        transform(fs, hs, 2 * i, 2 * i + 1)

    sign = (1 - 2 * lax.rem(lax.broadcasted_iota(jnp.int32, (64, Q), 0), 2)).astype(f32)

    @pl.loop(0, ROWS // 64)
    def _(r):
        up_rows = pl.ds(pl.multiple_of(r * 64, 64), 64)
        low_rows = pl.ds(pl.multiple_of(ROWS + r * 64, 64), 64)
        spec = [(hs[lag, up_rows], hs[lag, low_rows]) for lag in range(SEQ)]
        for lag in range(1, SEQ):
            hs[lag, up_rows] = spec[lag][0] - sign * spec[lag - 1][1]
            hs[lag, low_rows] = spec[lag][1] + sign * spec[lag - 1][0]

    for cp in z_copies:
        cp.wait_recv()
    total = zr[0].astype(f32)
    for i in range(1, ZS):
        total = total + zr[i].astype(f32)
    yr[y] = total.astype(bf16)
    y_copies = []
    for d in far_z:
        cp = remote(yr.at[y], yr.at[y], y_ss.at[d], y_rs.at[d], at_y(d))
        cp.start()
        y_copies.append(cp)

    g_by = dict(zip(far_seq, g_copies, strict=True))

    def from_seq(d):
        return lax.rem(s - d + SEQ, SEQ)

    g_by[1].wait_recv()
    transform(gs, xf, s, from_seq(1))
    g_by[3].wait_recv()
    g_by[2].wait_recv()
    transform(gs, xf, from_seq(3), from_seq(2))
    r_copies = []
    for pair in ((2, 1), (3, 0)):
        blocks = [lax.rem(s + d, SEQ) for d in pair]

        @pl.loop(0, ROWS // 64)
        def _(r):
            up_rows = pl.ds(pl.multiple_of(r * 64, 64), 64)
            low_rows = pl.ds(pl.multiple_of(ROWS + r * 64, 64), 64)
            for side, j in enumerate(blocks):

                def add(i, sums):
                    a, b = xf[i, up_rows], xf[i, low_rows]
                    p, q = hs[i - j, up_rows], hs[i - j, low_rows]
                    return sums[0] + a * p + b * q, sums[1] + b * p - a * q

                zeros = jnp.zeros((64, Q), f32)
                yre, yim = lax.fori_loop(j, SEQ, add, (zeros, zeros))
                ys[up_rows, side * Q : side * Q + Q] = yre.astype(bf16)
                ys[low_rows, side * Q : side * Q + Q] = yim.astype(bf16)

        spec = ys[...]
        out = (nn(itab[...], jnp.concatenate([spec, spec], axis=0)) * (1.0 / ROWS)).astype(bf16)
        for side, d in enumerate(pair):
            rs_send[d] = out[:, side * Q : side * Q + Q]
            if d:
                cp = remote(rs_send.at[d], gm_h.at[s], r_ss.at[d], r_rs.at[d], at_seq(d))
                r_copies.append(cp)
            else:
                cp = pltpu.make_async_copy(rs_send.at[d], gm_h.at[s], out_sem.at[1])
                out_copies.append(cp)
            cp.start()

    for cp in y_copies:
        cp.wait_recv()
    total = yr[0].astype(f32)
    for i in range(1, YS):
        total = total + yr[i].astype(f32)
    fin[...] = (total * factor).astype(bf16)
    n_copies = []
    for d in far_z:
        cp = remote(fin, fin_h.at[z], n_ss.at[d], n_rs.at[d], at_z(d))
        cp.start()
        n_copies.append(cp)

    out_copies.append(pltpu.make_async_copy(fin, fin_h.at[z], out_sem.at[2]))
    out_copies[-1].start()

    for cp in r_copies + n_copies:
        cp.wait_recv()
    for cp in [core_a, core_b] + f_copies + x_copies + g_copies + z_copies + y_copies + r_copies + n_copies:
        cp.wait_send()
    for cp in out_copies:
        cp.wait()


def results_kernel(
    gm_h, gx2_h, fin_h, values_h, first_h, x1_h, val_h, x2_h, a_h, b_h,
    gm, values, first, x1, val, x2, fin, low, in_sem, out_sem,
):
    halves = [pl.ds(0, ROWS // 2), pl.ds(ROWS // 2, ROWS // 2)]
    loads = []
    stores = []

    def fetch(src, dst):
        loads.append(pltpu.make_async_copy(src, dst, in_sem.at[len(loads)]))
        loads[-1].start()

    def put(src, dst):
        stores.append(pltpu.make_async_copy(src, dst, out_sem.at[len(stores)]))
        stores[-1].start()

    for rows in halves:
        fetch(gm_h.at[:, rows], gm.at[:, rows])
        fetch(values_h.at[rows], values.at[rows])
        fetch(first_h.at[rows], first.at[rows])
    fetch(gx2_h, x2)
    fetch(fin_h, fin)
    for i, rows in enumerate(halves):
        for cp in loads[3 * i : 3 * i + 3]:
            cp.wait()
        for q in range(SEQ):
            cols = slice(q * Q, q * Q + Q)
            mixed = gm[q, rows].astype(f32)
            x1[rows, cols] = (mixed * values[rows, cols].astype(f32)).astype(bf16)
            val[rows, cols] = (mixed * first[rows, cols].astype(f32)).astype(bf16)
        put(x1.at[rows], x1_h.at[rows])
        put(val.at[rows], val_h.at[rows])
    for cp in loads[6:]:
        cp.wait()
    put(x2, x2_h)
    for i in range(ZS):
        low[SL * i : SL * (i + 1)] = fin[i].astype(f32)
    put(low.at[pl.ds(0, RANK)], a_h)
    put(low.at[pl.ds(RANK, RANK)], b_h)
    for cp in stores:
        cp.wait()


def on_device(
    first_gate_1, operator_values, second_gate_2, convolved_output, output_gradient,
    frozen_gradient, filt, adapter_down_weight, adapter_up_weight,
):
    positions = lax.axis_size("win") * first_gate_1.shape[0] * first_gate_1.shape[1] * lax.axis_size("seq")
    factor = 2.0 / math.sqrt(positions)
    table = fourier_table()
    tab = jnp.asarray(np.concatenate(in_two(table), axis=1))
    itab = jnp.asarray(np.concatenate(in_two(np.ascontiguousarray(table.T)), axis=1))
    blk = functools.partial(pltpu.VMEM, (ROWS, CH))
    dma = pltpu.SemaphoreType.DMA
    mixed, grad_x2, slices = pl.pallas_call(
        functools.partial(kernel, factor),
        out_shape=(
            jax.ShapeDtypeStruct((SEQ, ROWS, Q), bf16),
            jax.ShapeDtypeStruct((ROWS, CH), bf16),
            jax.ShapeDtypeStruct((ZS, SL, CH), bf16),
        ),
        in_specs=[pl.BlockSpec(memory_space=pltpu.HBM)] * 9,
        out_specs=tuple([pl.BlockSpec(memory_space=pltpu.HBM)] * 3),
        scratch_shapes=[
            blk(bf16), blk(bf16), blk(bf16), blk(bf16), blk(bf16),
            pltpu.VMEM((RANK, CH), bf16), pltpu.VMEM((RANK, CH), bf16),
            pltpu.VMEM((2 * ROWS, 2 * ROWS), bf16), pltpu.VMEM((ROWS, 4 * ROWS), bf16),
            blk(bf16),
            blk(bf16),
            pltpu.VMEM((2, 128, 128), f32), pltpu.VMEM((128, 128), f32),
            pltpu.VMEM((XS, 128, 128), bf16), pltpu.VMEM((2, 128, 128), bf16),
            pltpu.VMEM((SEQ, ROWS, Q), bf16),
            pltpu.VMEM((SEQ - 1, ROWS, Q), bf16), pltpu.VMEM((SEQ, ROWS, Q), bf16),
            pltpu.VMEM((SEQ, 2 * ROWS, Q), f32), pltpu.VMEM((SEQ, 2 * ROWS, Q), f32),
            pltpu.VMEM((2 * ROWS, 2 * Q), bf16),
            pltpu.VMEM((SEQ, ROWS, Q), bf16),
            pltpu.VMEM((ZS, SL, CH), bf16), pltpu.VMEM((ZS, SL, CH), bf16),
            pltpu.VMEM((YS, SL, CH), bf16), pltpu.VMEM((SL, CH), bf16),
            dma((9,)), dma((2,)), dma((2,)), dma((XS,)), dma((XS,)),
            dma((SEQ,)), dma((SEQ,)), dma((SEQ,)), dma((SEQ,)), dma((SEQ,)), dma((SEQ,)),
            dma((ZS,)), dma((ZS,)), dma((YS,)), dma((YS,)), dma((ZS,)), dma((ZS,)), dma((3,)),
            pltpu.SemaphoreType.REGULAR,
        ],
        compiler_params=pltpu.CompilerParams(
            collective_id=0, has_side_effects=True, vmem_limit_bytes=60 * 1024 * 1024
        ),
        name="window_backward",
    )(
        second_gate_2[0], convolved_output[0], output_gradient[0], frozen_gradient[0], filt,
        adapter_down_weight.T, adapter_up_weight, tab, itab,
    )
    wide = jax.ShapeDtypeStruct((ROWS, CH), bf16)
    low = jax.ShapeDtypeStruct((RANK, CH), f32)
    grad_x1, grad_values, grad_x2, grad_a, grad_b = pl.pallas_call(
        results_kernel,
        out_shape=(wide, wide, wide, low, low),
        in_specs=[pl.BlockSpec(memory_space=pl.ANY)] * 5,
        out_specs=tuple([pl.BlockSpec(memory_space=pl.ANY)] * 5),
        scratch_shapes=[pltpu.VMEM((SEQ, ROWS, Q), bf16)] + [blk(bf16)] * 5
        + [pltpu.VMEM((ZS, SL, CH), bf16), pltpu.VMEM((2 * RANK, CH), f32), dma((8,)), dma((7,))],
        compiler_params=pltpu.CompilerParams(vmem_limit_bytes=60 * 1024 * 1024),
        name="results",
    )(mixed, grad_x2, slices, operator_values[0], first_gate_1[0])
    return grad_x1[None], grad_values[None], grad_x2[None], grad_a.T, grad_b


def solution(mesh):
    block = P("win", "seq", "chan")
    in_specs = (block,) * 6 + (P("seq", "chan"), P("chan", None), P(None, "chan"))
    out_specs = (block,) * 3 + (P("chan", None), P(None, "chan"))
    return jax.shard_map(
        on_device, mesh=mesh, in_specs=in_specs, out_specs=out_specs, check_vma=False
    )
```

```python
import functools
import math

import jax
import jax.numpy as jnp
import ml_dtypes
import numpy as np
from jax import lax
from jax.experimental import pallas as pl
from jax.experimental.pallas import tpu as pltpu
from jax.sharding import PartitionSpec as P

MESH = pl.DeviceIdType.MESH
bf16 = jnp.bfloat16
f32 = jnp.float32

ROWS = 256
CH = 512
Q = 128
RANK = 64
SEQ = 4
XS = 4
ZS = 8
YS = 8
SL = 2 * RANK // ZS


def fourier_table():
    k = np.arange(ROWS)[:, None]
    t = np.arange(ROWS)[None, :]
    angle = 2.0 * math.pi / (2 * ROWS) * ((2 * k + 1) * t % (4 * ROWS)) / 2.0
    return np.concatenate([np.cos(angle), -np.sin(angle)], axis=0)


def in_two(table):
    high = table.astype(ml_dtypes.bfloat16)
    return high, (table - high.astype(np.float64)).astype(ml_dtypes.bfloat16)


def nt(a, b):
    return lax.dot_general(a, b, (((1,), (1,)), ((), ())), preferred_element_type=f32)


def nn(a, b):
    return lax.dot_general(a, b, (((1,), (0,)), ((), ())), preferred_element_type=f32)


def tn(a, b):
    return lax.dot_general(a, b, (((0,), (0,)), ((), ())), preferred_element_type=f32)


def lanes(i):
    return pl.ds(pl.multiple_of(i * Q, Q), Q)


def kernel(
    factor,
    second_h, conv_h, og_h, frozen_h, filt_h, down_h, up_h, tab_h, itab_h,
    gm_h, gx2_h, fin_h,
    second, conv, og, frozen, filt, down, up, tab, itab,
    gx2, gated, pq, pq_in, xs, pqb, fs, gs_send, gs, hs, xf, ys, rs_send,
    ab_send, zr, yr, fin,
    load_sem, core_ss, core_rs, x_ss, x_rs, f_ss, f_rs, g_ss, g_rs, r_ss, r_rs, z_ss, z_rs, y_ss, y_rs, n_ss, n_rs, out_sem, answer_sem,
):
    w = lax.axis_index("win")
    s = lax.axis_index("seq")
    c = lax.axis_index("chan")
    ylo, z = w // ZS, lax.rem(w, ZS)
    y = s * 2 + ylo
    x, core = c // 2, lax.rem(c, 2)

    def at_core():
        return (w, s, x * 2 + 1 - core)

    def at_x(d):
        return (w, s, lax.rem(x + d, XS) * 2 + core)

    def at_seq(d):
        return (w, lax.rem(s + d, SEQ), c)

    def at_z(d):
        return (ylo * ZS + lax.rem(z + d, ZS), s, c)

    def at_y(d):
        other = lax.rem(y + d, YS)
        return (lax.rem(other, 2) * ZS + z, other // 2, c)

    far_x = (2, 1, 3)
    far_seq = (2, 1, 3)
    far_z = (4, 3, 5, 2, 6, 1, 7)
    partners = [at_core()] + [at_x(d) for d in far_x] + [at_y(d) for d in far_z]
    barrier = pltpu.get_barrier_semaphore()

    def greet(semaphore, wanted):
        for d in far_z:
            @pl.when(wanted(lax.rem(z + d, ZS)))
            def _():
                pl.semaphore_signal(semaphore, inc=1, device_id=at_z(d), device_id_type=MESH)

    greet(barrier, lambda other: other > z)
    for p in partners:
        pl.semaphore_signal(barrier, inc=1, device_id=p, device_id_type=MESH)

    loads = {}
    pairs = (
        ("og", og_h, og), ("up", up_h, up), ("second", second_h, second), ("conv", conv_h, conv),
        ("down", down_h, down), ("filt", filt_h, filt), ("frozen", frozen_h, frozen),
        ("tab", tab_h, tab), ("itab", itab_h, itab),
    )
    for i, (name, src, dst) in enumerate(pairs):
        loads[name] = pltpu.make_async_copy(src, dst, load_sem.at[i])
        loads[name].start()

    def remote(src, dst, ss, rs_, dev):
        return pltpu.make_async_remote_copy(
            src_ref=src, dst_ref=dst, send_sem=ss, recv_sem=rs_, device_id=dev, device_id_type=MESH
        )

    def keep(part, base):
        for half in range(2):
            pq[half, base : base + RANK] = part[:, half * 128 : half * 128 + 128]

    loads["og"].wait()
    loads["up"].wait()
    keep(nt(up[...], og[...]), 0)
    loads["second"].wait()
    loads["conv"].wait()
    loads["down"].wait()
    gated[...] = (second[...].astype(f32) * conv[...].astype(f32)).astype(bf16)
    keep(nt(down[...], gated[...]), RANK)
    loads["filt"].wait()

    pl.semaphore_wait(barrier, len(partners) + z)
    greet(answer_sem, lambda other: other < z)

    core_a = remote(pq.at[1 - core], pq_in, core_ss.at[0], core_rs.at[0], at_core())
    core_a.start()
    f_copies = []
    for d in far_seq:
        cp = remote(filt.at[:, lanes(lax.rem(s + d, SEQ))], fs.at[s], f_ss.at[d], f_rs.at[d], at_seq(d))
        cp.start()
        f_copies.append(cp)
    core_a.wait_recv()
    xs[x] = (pq[core] + pq_in[...]).astype(bf16)
    x_copies = []
    for d in far_x:
        cp = remote(xs.at[x], xs.at[x], x_ss.at[d], x_rs.at[d], at_x(d))
        cp.start()
        x_copies.append(cp)
    fs[s] = filt[:, lanes(s)]
    for n in ("frozen", "tab", "itab"):
        loads[n].wait()
    for cp in x_copies:
        cp.wait_recv()
    parts = [xs[i].astype(f32) for i in range(XS)]
    pqb[core] = ((parts[0] + parts[1]) + (parts[2] + parts[3])).astype(bf16)
    core_b = remote(pqb.at[core], pqb.at[core], core_ss.at[1], core_rs.at[1], at_core())
    core_b.start()
    core_b.wait_recv()

    low_back, low_in = (
        jnp.concatenate([pqb[0, base : base + RANK], pqb[1, base : base + RANK]], axis=1) for base in (0, RANK)
    )

    def grad_conv(q):
        gg = frozen[:, lanes(q)].astype(f32) + 2.0 * tn(low_back, down[:, lanes(q)])
        gx2[:, lanes(q)] = (gg * conv[:, lanes(q)].astype(f32)).astype(bf16)
        return (gg * second[:, lanes(q)].astype(f32)).astype(bf16)

    part_a = nn(low_back, gated[...]).astype(bf16)
    part_b = nn(low_in, og[...]).astype(bf16)
    for i in range(ZS // 2):
        ab_send[i] = part_a[SL * i : SL * (i + 1)]
        ab_send[ZS // 2 + i] = part_b[SL * i : SL * (i + 1)]

    @pl.when(z < ZS - 1)
    def _():
        pl.semaphore_wait(answer_sem, ZS - 1 - z)

    z_copies = []
    for d in far_z:
        cp = remote(ab_send.at[lax.rem(z + d, ZS)], zr.at[z], z_ss.at[d], z_rs.at[d], at_z(d))
        cp.start()
        z_copies.append(cp)
    zr[z] = ab_send[z]
    g_copies = [
        remote(gs_send.at[i], gs.at[s], g_ss.at[d], g_rs.at[d], at_seq(d)) for i, d in enumerate(far_seq)
    ]
    r_copies = [
        remote(rs_send.at[d], gm_h.at[s], r_ss.at[d], r_rs.at[d], at_seq(d)) for d in far_seq
    ]
    out_copies = [
        pltpu.make_async_copy(gx2, gx2_h, out_sem.at[0]),
        pltpu.make_async_copy(rs_send.at[0], gm_h.at[s], out_sem.at[1]),
        pltpu.make_async_copy(fin, fin_h.at[z], out_sem.at[2]),
    ]

    def send_grad_conv():
        for i, (d, cp) in enumerate(zip(far_seq, g_copies, strict=True)):
            gs_send[i] = grad_conv(lax.rem(s + d, SEQ))
            cp.start()
        gs[s] = grad_conv(s)
        out_copies[0].start()

    def transform(src, dst, i, j):
        both = jnp.concatenate([src[i], src[j]], axis=1)
        spec = nn(tab[...], jnp.concatenate([both, both], axis=0))
        dst[i] = spec[:, :Q]
        dst[j] = spec[:, Q:]

    g_by = dict(zip(far_seq, g_copies, strict=True))
    r_by = dict(zip(far_seq, r_copies, strict=True))

    def from_seq(d):
        return lax.rem(s - d + SEQ, SEQ)

    def convolve():
        g_by[1].wait_recv()
        transform(gs, xf, s, from_seq(1))
        g_by[3].wait_recv()
        g_by[2].wait_recv()
        transform(gs, xf, from_seq(3), from_seq(2))
        for pair in ((2, 1), (3, 0)):
            blocks = [lax.rem(s + d, SEQ) for d in pair]

            @pl.loop(0, ROWS // 64)
            def _(r):
                up_rows = pl.ds(pl.multiple_of(r * 64, 64), 64)
                low_rows = pl.ds(pl.multiple_of(ROWS + r * 64, 64), 64)
                for side, j in enumerate(blocks):

                    def add(i, sums):
                        a, b = xf[i, up_rows], xf[i, low_rows]
                        p, q = hs[i - j, up_rows], hs[i - j, low_rows]
                        return sums[0] + a * p + b * q, sums[1] + b * p - a * q

                    zeros = jnp.zeros((64, Q), f32)
                    yre, yim = lax.fori_loop(j, SEQ, add, (zeros, zeros))
                    ys[up_rows, side * Q : side * Q + Q] = yre.astype(bf16)
                    ys[low_rows, side * Q : side * Q + Q] = yim.astype(bf16)

            spec = ys[...]
            out = (nn(itab[...], jnp.concatenate([spec, spec], axis=0)) * (1.0 / ROWS)).astype(bf16)
            for side, d in enumerate(pair):
                rs_send[d] = out[:, side * Q : side * Q + Q]
                (r_by[d] if d else out_copies[1]).start()

    pl.when(z < 8)(send_grad_conv)

    for cp in f_copies:
        cp.wait_recv()

    @pl.loop(0, SEQ // 2)
    def _(i):
        transform(fs, hs, 2 * i, 2 * i + 1)

    sign = (1 - 2 * lax.rem(lax.broadcasted_iota(jnp.int32, (64, Q), 0), 2)).astype(f32)

    @pl.loop(0, ROWS // 64)
    def _(r):
        up_rows = pl.ds(pl.multiple_of(r * 64, 64), 64)
        low_rows = pl.ds(pl.multiple_of(ROWS + r * 64, 64), 64)
        spec = [(hs[lag, up_rows], hs[lag, low_rows]) for lag in range(SEQ)]
        for lag in range(1, SEQ):
            hs[lag, up_rows] = spec[lag][0] - sign * spec[lag - 1][1]
            hs[lag, low_rows] = spec[lag][1] + sign * spec[lag - 1][0]

    for cp in z_copies:
        cp.wait_recv()
    total = zr[0].astype(f32)
    for i in range(1, ZS):
        total = total + zr[i].astype(f32)
    yr[y] = total.astype(bf16)
    y_copies = []
    for d in far_z:
        cp = remote(yr.at[y], yr.at[y], y_ss.at[d], y_rs.at[d], at_y(d))
        cp.start()
        y_copies.append(cp)

    pl.when((z >= 0) & (z < 4))(convolve)
    for cp in y_copies:
        cp.wait_recv()
    total = yr[0].astype(f32)
    for i in range(1, YS):
        total = total + yr[i].astype(f32)
    fin[...] = (total * factor).astype(bf16)
    n_copies = []
    for d in far_z:
        cp = remote(fin, fin_h.at[z], n_ss.at[d], n_rs.at[d], at_z(d))
        cp.start()
        n_copies.append(cp)

    out_copies[2].start()

    pl.when(z >= 4)(convolve)

    for cp in r_copies + n_copies:
        cp.wait_recv()
    for cp in [core_a, core_b] + f_copies + x_copies + g_copies + z_copies + y_copies + r_copies + n_copies:
        cp.wait_send()
    for cp in out_copies:
        cp.wait()


def results_kernel(
    gm_h, gx2_h, fin_h, values_h, first_h, x1_h, val_h, x2_h, a_h, b_h,
    gm, values, first, x1, val, x2, fin, low, in_sem, out_sem,
):
    parts = 2
    halves = [pl.ds(ROWS // parts * i, ROWS // parts) for i in range(parts)]
    loads = []
    stores = []

    def fetch(src, dst):
        loads.append(pltpu.make_async_copy(src, dst, in_sem.at[len(loads)]))
        loads[-1].start()

    def put(src, dst):
        stores.append(pltpu.make_async_copy(src, dst, out_sem.at[len(stores)]))
        stores[-1].start()

    fetch(gx2_h, x2)
    fetch(fin_h, fin)
    for rows in halves:
        fetch(gm_h.at[:, rows], gm.at[:, rows])
        fetch(values_h.at[rows], values.at[rows])
        fetch(first_h.at[rows], first.at[rows])
    for cp in loads[:2]:
        cp.wait()
    put(x2, x2_h)
    for i in range(ZS):
        low[SL * i : SL * (i + 1)] = fin[i].astype(f32)
    put(low.at[pl.ds(0, RANK)], a_h)
    put(low.at[pl.ds(RANK, RANK)], b_h)
    for i, rows in enumerate(halves):
        for cp in loads[3 * i + 2 : 3 * i + 5]:
            cp.wait()
        for q in range(SEQ):
            cols = slice(q * Q, q * Q + Q)
            mixed = gm[q, rows].astype(f32)
            x1[rows, cols] = (mixed * values[rows, cols].astype(f32)).astype(bf16)
            val[rows, cols] = (mixed * first[rows, cols].astype(f32)).astype(bf16)
        put(x1.at[rows], x1_h.at[rows])
        put(val.at[rows], val_h.at[rows])
    for cp in stores:
        cp.wait()


def on_device(
    first_gate_1, operator_values, second_gate_2, convolved_output, output_gradient,
    frozen_gradient, filt, adapter_down_weight, adapter_up_weight,
):
    positions = lax.axis_size("win") * first_gate_1.shape[0] * first_gate_1.shape[1] * lax.axis_size("seq")
    factor = 2.0 / math.sqrt(positions)
    table = fourier_table()
    tab = jnp.asarray(np.concatenate(in_two(table), axis=1))
    itab = jnp.asarray(np.concatenate(in_two(np.ascontiguousarray(table.T)), axis=1))
    blk = functools.partial(pltpu.VMEM, (ROWS, CH))
    dma = pltpu.SemaphoreType.DMA
    mixed, grad_x2, slices = pl.pallas_call(
        functools.partial(kernel, factor),
        out_shape=(
            jax.ShapeDtypeStruct((SEQ, ROWS, Q), bf16),
            jax.ShapeDtypeStruct((ROWS, CH), bf16),
            jax.ShapeDtypeStruct((ZS, SL, CH), bf16),
        ),
        in_specs=[pl.BlockSpec(memory_space=pltpu.HBM)] * 9,
        out_specs=tuple([pl.BlockSpec(memory_space=pltpu.HBM)] * 3),
        scratch_shapes=[
            blk(bf16), blk(bf16), blk(bf16), blk(bf16), blk(bf16),
            pltpu.VMEM((RANK, CH), bf16), pltpu.VMEM((RANK, CH), bf16),
            pltpu.VMEM((2 * ROWS, 2 * ROWS), bf16), pltpu.VMEM((ROWS, 4 * ROWS), bf16),
            blk(bf16),
            blk(bf16),
            pltpu.VMEM((2, 128, 128), f32), pltpu.VMEM((128, 128), f32),
            pltpu.VMEM((XS, 128, 128), bf16), pltpu.VMEM((2, 128, 128), bf16),
            pltpu.VMEM((SEQ, ROWS, Q), bf16),
            pltpu.VMEM((SEQ - 1, ROWS, Q), bf16), pltpu.VMEM((SEQ, ROWS, Q), bf16),
            pltpu.VMEM((SEQ, 2 * ROWS, Q), f32), pltpu.VMEM((SEQ, 2 * ROWS, Q), f32),
            pltpu.VMEM((2 * ROWS, 2 * Q), bf16),
            pltpu.VMEM((SEQ, ROWS, Q), bf16),
            pltpu.VMEM((ZS, SL, CH), bf16), pltpu.VMEM((ZS, SL, CH), bf16),
            pltpu.VMEM((YS, SL, CH), bf16), pltpu.VMEM((SL, CH), bf16),
            dma((9,)), dma((2,)), dma((2,)), dma((XS,)), dma((XS,)),
            dma((SEQ,)), dma((SEQ,)), dma((SEQ,)), dma((SEQ,)), dma((SEQ,)), dma((SEQ,)),
            dma((ZS,)), dma((ZS,)), dma((YS,)), dma((YS,)), dma((ZS,)), dma((ZS,)), dma((3,)),
            pltpu.SemaphoreType.REGULAR,
        ],
        compiler_params=pltpu.CompilerParams(
            collective_id=0, has_side_effects=True, vmem_limit_bytes=60 * 1024 * 1024
        ),
        name="window_backward",
    )(
        second_gate_2[0], convolved_output[0], output_gradient[0], frozen_gradient[0], filt,
        adapter_down_weight.T, adapter_up_weight, tab, itab,
    )
    wide = jax.ShapeDtypeStruct((ROWS, CH), bf16)
    low = jax.ShapeDtypeStruct((RANK, CH), f32)
    grad_x1, grad_values, grad_x2, grad_a, grad_b = pl.pallas_call(
        results_kernel,
        out_shape=(wide, wide, wide, low, low),
        in_specs=[pl.BlockSpec(memory_space=pl.ANY)] * 5,
        out_specs=tuple([pl.BlockSpec(memory_space=pl.ANY)] * 5),
        scratch_shapes=[pltpu.VMEM((SEQ, ROWS, Q), bf16)] + [blk(bf16)] * 5
        + [pltpu.VMEM((ZS, SL, CH), bf16), pltpu.VMEM((2 * RANK, CH), f32), dma((8,)), dma((7,))],
        compiler_params=pltpu.CompilerParams(vmem_limit_bytes=60 * 1024 * 1024),
        name="results",
    )(mixed, grad_x2, slices, operator_values[0], first_gate_1[0])
    return grad_x1[None], grad_values[None], grad_x2[None], grad_a.T, grad_b


def solution(mesh):
    block = P("win", "seq", "chan")
    in_specs = (block,) * 6 + (P("seq", "chan"), P("chan", None), P(None, "chan"))
    out_specs = (block,) * 3 + (P("chan", None), P(None, "chan"))
    return jax.shard_map(
        on_device, mesh=mesh, in_specs=in_specs, out_specs=out_specs, check_vma=False
    )
```

```python
import functools
import math

import jax
import jax.numpy as jnp
import ml_dtypes
import numpy as np
from jax import lax
from jax.experimental import pallas as pl
from jax.experimental.pallas import tpu as pltpu
from jax.sharding import PartitionSpec as P

MESH = pl.DeviceIdType.MESH
bf16 = jnp.bfloat16
f32 = jnp.float32

ROWS = 256
CH = 512
Q = 128
RANK = 64
SEQ = 4
XS = 4
ZS = 8
YS = 8
SL = 2 * RANK // ZS


def fourier_table():
    k = np.arange(ROWS)[:, None]
    t = np.arange(ROWS)[None, :]
    angle = 2.0 * math.pi / (2 * ROWS) * ((2 * k + 1) * t % (4 * ROWS)) / 2.0
    return np.concatenate([np.cos(angle), -np.sin(angle)], axis=0)


def in_two(table):
    high = table.astype(ml_dtypes.bfloat16)
    return high, (table - high.astype(np.float64)).astype(ml_dtypes.bfloat16)


def nt(a, b):
    return lax.dot_general(a, b, (((1,), (1,)), ((), ())), preferred_element_type=f32)


def nn(a, b):
    return lax.dot_general(a, b, (((1,), (0,)), ((), ())), preferred_element_type=f32)


def tn(a, b):
    return lax.dot_general(a, b, (((0,), (0,)), ((), ())), preferred_element_type=f32)


def lanes(i):
    return pl.ds(pl.multiple_of(i * Q, Q), Q)


def kernel(
    factor,
    second_h, conv_h, og_h, frozen_h, filt_h, down_h, up_h, tab_h, itab_h,
    gm_h, gx2_h, fin_h,
    second, conv, og, frozen, filt, down, up, tab, itab,
    gx2, gated, pq, pq_in, xs, pqb, fs, gs_send, gs, hs, xf, ys, rs_send,
    ab_send, zr, yr, fin,
    load_sem, core_ss, core_rs, x_ss, x_rs, f_ss, f_rs, g_ss, g_rs, r_ss, r_rs, z_ss, z_rs, y_ss, y_rs, n_ss, n_rs, out_sem, answer_sem,
):
    w = lax.axis_index("win")
    s = lax.axis_index("seq")
    c = lax.axis_index("chan")
    ylo, z = w // ZS, lax.rem(w, ZS)
    y = s * 2 + ylo
    x, core = c // 2, lax.rem(c, 2)

    def at_core():
        return (w, s, x * 2 + 1 - core)

    def at_x(d):
        return (w, s, lax.rem(x + d, XS) * 2 + core)

    def at_seq(d):
        return (w, lax.rem(s + d, SEQ), c)

    def at_z(d):
        return (ylo * ZS + lax.rem(z + d, ZS), s, c)

    def at_y(d):
        other = lax.rem(y + d, YS)
        return (lax.rem(other, 2) * ZS + z, other // 2, c)

    far_x = (2, 1, 3)
    far_seq = (2, 1, 3)
    far_z = (4, 3, 5, 2, 6, 1, 7)
    loads = {}
    pairs = (
        ("og", og_h, og), ("up", up_h, up), ("second", second_h, second), ("conv", conv_h, conv),
        ("down", down_h, down), ("filt", filt_h, filt), ("frozen", frozen_h, frozen),
        ("tab", tab_h, tab), ("itab", itab_h, itab),
    )
    for i, (name, src, dst) in enumerate(pairs):
        loads[name] = pltpu.make_async_copy(src, dst, load_sem.at[i])
        loads[name].start()

    partners = [at_core()] + [at_x(d) for d in far_x] + [at_y(d) for d in far_z]
    barrier = pltpu.get_barrier_semaphore()

    def greet(semaphore, wanted):
        for d in far_z:
            @pl.when(wanted(lax.rem(z + d, ZS)))
            def _():
                pl.semaphore_signal(semaphore, inc=1, device_id=at_z(d), device_id_type=MESH)

    greet(barrier, lambda other: other > z)
    for p in partners:
        pl.semaphore_signal(barrier, inc=1, device_id=p, device_id_type=MESH)

    def remote(src, dst, ss, rs_, dev):
        return pltpu.make_async_remote_copy(
            src_ref=src, dst_ref=dst, send_sem=ss, recv_sem=rs_, device_id=dev, device_id_type=MESH
        )

    def keep(part, base):
        for half in range(2):
            pq[half, base : base + RANK] = part[:, half * 128 : half * 128 + 128]

    loads["og"].wait()
    loads["up"].wait()
    keep(nt(up[...], og[...]), 0)
    loads["second"].wait()
    loads["conv"].wait()
    loads["down"].wait()
    gated[...] = (second[...].astype(f32) * conv[...].astype(f32)).astype(bf16)
    keep(nt(down[...], gated[...]), RANK)
    loads["filt"].wait()

    pl.semaphore_wait(barrier, len(partners) + z)
    greet(answer_sem, lambda other: other < z)

    core_a = remote(pq.at[1 - core], pq_in, core_ss.at[0], core_rs.at[0], at_core())
    core_a.start()
    f_copies = []
    for d in far_seq:
        cp = remote(filt.at[:, lanes(lax.rem(s + d, SEQ))], fs.at[s], f_ss.at[d], f_rs.at[d], at_seq(d))
        cp.start()
        f_copies.append(cp)
    core_a.wait_recv()
    xs[x] = (pq[core] + pq_in[...]).astype(bf16)
    x_copies = []
    for d in far_x:
        cp = remote(xs.at[x], xs.at[x], x_ss.at[d], x_rs.at[d], at_x(d))
        cp.start()
        x_copies.append(cp)
    fs[s] = filt[:, lanes(s)]
    for n in ("frozen", "tab", "itab"):
        loads[n].wait()
    for cp in x_copies:
        cp.wait_recv()
    parts = [xs[i].astype(f32) for i in range(XS)]
    pqb[core] = ((parts[0] + parts[1]) + (parts[2] + parts[3])).astype(bf16)
    core_b = remote(pqb.at[core], pqb.at[core], core_ss.at[1], core_rs.at[1], at_core())
    core_b.start()
    core_b.wait_recv()

    low_back, low_in = (
        jnp.concatenate([pqb[0, base : base + RANK], pqb[1, base : base + RANK]], axis=1) for base in (0, RANK)
    )

    def grad_conv(q):
        gg = frozen[:, lanes(q)].astype(f32) + 2.0 * tn(low_back, down[:, lanes(q)])
        gx2[:, lanes(q)] = (gg * conv[:, lanes(q)].astype(f32)).astype(bf16)
        return (gg * second[:, lanes(q)].astype(f32)).astype(bf16)

    part_a = nn(low_back, gated[...]).astype(bf16)
    part_b = nn(low_in, og[...]).astype(bf16)
    for i in range(ZS // 2):
        ab_send[i] = part_a[SL * i : SL * (i + 1)]
        ab_send[ZS // 2 + i] = part_b[SL * i : SL * (i + 1)]

    @pl.when(z < ZS - 1)
    def _():
        pl.semaphore_wait(answer_sem, ZS - 1 - z)

    z_copies = []
    for d in far_z:
        cp = remote(ab_send.at[lax.rem(z + d, ZS)], zr.at[z], z_ss.at[d], z_rs.at[d], at_z(d))
        cp.start()
        z_copies.append(cp)
    zr[z] = ab_send[z]
    g_copies = [
        remote(gs_send.at[i], gs.at[s], g_ss.at[d], g_rs.at[d], at_seq(d)) for i, d in enumerate(far_seq)
    ]
    r_copies = [
        remote(rs_send.at[d], gm_h.at[s], r_ss.at[d], r_rs.at[d], at_seq(d)) for d in far_seq
    ]
    out_copies = [
        pltpu.make_async_copy(gx2, gx2_h, out_sem.at[0]),
        pltpu.make_async_copy(rs_send.at[0], gm_h.at[s], out_sem.at[1]),
        pltpu.make_async_copy(fin, fin_h.at[z], out_sem.at[2]),
    ]

    @pl.loop(0, SEQ - 1)
    def _(i):
        d = jnp.where(i == SEQ - 2, SEQ - 1, 2 - i)
        gs_send[i] = grad_conv(lax.rem(s + d, SEQ))
        remote(gs_send.at[i], gs.at[s], g_ss.at[d], g_rs.at[d], at_seq(d)).start()

    gs[s] = grad_conv(s)
    out_copies[0].start()

    def transform(src, dst, i, j):
        both = jnp.concatenate([src[i], src[j]], axis=1)
        spec = nn(tab[...], jnp.concatenate([both, both], axis=0))
        dst[i] = spec[:, :Q]
        dst[j] = spec[:, Q:]

    g_by = dict(zip(far_seq, g_copies, strict=True))
    r_by = dict(zip(far_seq, r_copies, strict=True))

    def from_seq(d):
        return lax.rem(s - d + SEQ, SEQ)

    def convolve():
        @pl.loop(0, 2)
        def _(i):
            @pl.when(i == 0)
            def _():
                g_by[1].wait_recv()

            @pl.when(i == 1)
            def _():
                g_by[3].wait_recv()
                g_by[2].wait_recv()

            transform(gs, xf, from_seq(3 * i), from_seq(1 + i))

        @pl.loop(0, 2)
        def _(step):
            pair = (2 + step, 1 - step)
            blocks = [lax.rem(s + d, SEQ) for d in pair]

            @pl.loop(0, ROWS // 64)
            def _(r):
                up_rows = pl.ds(pl.multiple_of(r * 64, 64), 64)
                low_rows = pl.ds(pl.multiple_of(ROWS + r * 64, 64), 64)
                for side, j in enumerate(blocks):

                    def add(i, sums):
                        a, b = xf[i, up_rows], xf[i, low_rows]
                        p, q = hs[i - j, up_rows], hs[i - j, low_rows]
                        return sums[0] + a * p + b * q, sums[1] + b * p - a * q

                    zeros = jnp.zeros((64, Q), f32)
                    yre, yim = lax.fori_loop(j, SEQ, add, (zeros, zeros))
                    ys[up_rows, side * Q : side * Q + Q] = yre.astype(bf16)
                    ys[low_rows, side * Q : side * Q + Q] = yim.astype(bf16)

            spec = ys[...]
            out = (nn(itab[...], jnp.concatenate([spec, spec], axis=0)) * (1.0 / ROWS)).astype(bf16)
            for side, d in enumerate(pair):
                rs_send[d] = out[:, side * Q : side * Q + Q]
            far, other = pair
            remote(rs_send.at[far], gm_h.at[s], r_ss.at[far], r_rs.at[far], at_seq(far)).start()

            @pl.when(step == 0)
            def _():
                r_by[1].start()

            @pl.when(step == 1)
            def _():
                out_copies[1].start()


    for cp in f_copies:
        cp.wait_recv()

    @pl.loop(0, SEQ // 2)
    def _(i):
        transform(fs, hs, 2 * i, 2 * i + 1)

    sign = (1 - 2 * lax.rem(lax.broadcasted_iota(jnp.int32, (64, Q), 0), 2)).astype(f32)

    @pl.loop(0, ROWS // 64)
    def _(r):
        up_rows = pl.ds(pl.multiple_of(r * 64, 64), 64)
        low_rows = pl.ds(pl.multiple_of(ROWS + r * 64, 64), 64)
        spec = [(hs[lag, up_rows], hs[lag, low_rows]) for lag in range(SEQ)]
        for lag in range(1, SEQ):
            hs[lag, up_rows] = spec[lag][0] - sign * spec[lag - 1][1]
            hs[lag, low_rows] = spec[lag][1] + sign * spec[lag - 1][0]

    y_copies = [remote(yr.at[y], yr.at[y], y_ss.at[d], y_rs.at[d], at_y(d)) for d in far_z]
    n_copies = [remote(fin, fin_h.at[z], n_ss.at[d], n_rs.at[d], at_z(d)) for d in far_z]

    def sum_z():
        for cp in z_copies:
            cp.wait_recv()
        total = zr[0].astype(f32)
        for i in range(1, ZS):
            total = total + zr[i].astype(f32)
        yr[y] = total.astype(bf16)
        for cp in y_copies:
            cp.start()

    def sum_y():
        for cp in y_copies:
            cp.wait_recv()
        total = yr[0].astype(f32)
        for i in range(1, YS):
            total = total + yr[i].astype(f32)
        fin[...] = (total * factor).astype(bf16)
        for cp in n_copies:
            cp.start()

        out_copies[2].start()

    convolution = jnp.where(z < 4, 1, 2)

    @pl.loop(0, 3)
    def _(step):
        pl.when(step == convolution)(convolve)
        pl.when(step == jnp.where(convolution == 0, 1, 0))(sum_z)
        pl.when(step == jnp.where(convolution == 2, 1, 2))(sum_y)

    for cp in [core_a, core_b] + f_copies + x_copies + g_copies + z_copies + y_copies + r_copies + n_copies:
        cp.wait_send()
    for cp in out_copies:
        cp.wait()
    for cp in r_copies + n_copies:
        cp.wait_recv()


def results_kernel(
    gm_h, gx2_h, fin_h, values_h, first_h, x1_h, val_h, x2_h, a_h, b_h,
    gm, values, first, x1, val, x2, fin, low, in_sem, out_sem,
):
    parts = 2
    halves = [pl.ds(ROWS // parts * i, ROWS // parts) for i in range(parts)]
    loads = []
    stores = []

    def fetch(src, dst):
        loads.append(pltpu.make_async_copy(src, dst, in_sem.at[len(loads)]))
        loads[-1].start()

    def put(src, dst):
        stores.append(pltpu.make_async_copy(src, dst, out_sem.at[len(stores)]))
        stores[-1].start()

    fetch(gx2_h, x2)
    fetch(fin_h, fin)
    for rows in halves:
        fetch(gm_h.at[:, rows], gm.at[:, rows])
        fetch(values_h.at[rows], values.at[rows])
        fetch(first_h.at[rows], first.at[rows])
    for cp in loads[:2]:
        cp.wait()
    put(x2, x2_h)
    for i in range(ZS):
        low[SL * i : SL * (i + 1)] = fin[i].astype(f32)
    put(low.at[pl.ds(0, RANK)], a_h)
    put(low.at[pl.ds(RANK, RANK)], b_h)
    for i, rows in enumerate(halves):
        for cp in loads[3 * i + 2 : 3 * i + 5]:
            cp.wait()
        for q in range(SEQ):
            cols = slice(q * Q, q * Q + Q)
            mixed = gm[q, rows].astype(f32)
            x1[rows, cols] = (mixed * values[rows, cols].astype(f32)).astype(bf16)
            val[rows, cols] = (mixed * first[rows, cols].astype(f32)).astype(bf16)
        put(x1.at[rows], x1_h.at[rows])
        put(val.at[rows], val_h.at[rows])
    for cp in stores:
        cp.wait()


def on_device(
    first_gate_1, operator_values, second_gate_2, convolved_output, output_gradient,
    frozen_gradient, filt, adapter_down_weight, adapter_up_weight,
):
    positions = lax.axis_size("win") * first_gate_1.shape[0] * first_gate_1.shape[1] * lax.axis_size("seq")
    factor = 2.0 / math.sqrt(positions)
    table = fourier_table()
    tab = jnp.asarray(np.concatenate(in_two(table), axis=1))
    itab = jnp.asarray(np.concatenate(in_two(np.ascontiguousarray(table.T)), axis=1))
    blk = functools.partial(pltpu.VMEM, (ROWS, CH))
    dma = pltpu.SemaphoreType.DMA
    mixed, grad_x2, slices = pl.pallas_call(
        functools.partial(kernel, factor),
        out_shape=(
            jax.ShapeDtypeStruct((SEQ, ROWS, Q), bf16),
            jax.ShapeDtypeStruct((ROWS, CH), bf16),
            jax.ShapeDtypeStruct((ZS, SL, CH), bf16),
        ),
        in_specs=[pl.BlockSpec(memory_space=pltpu.HBM)] * 9,
        out_specs=tuple([pl.BlockSpec(memory_space=pltpu.HBM)] * 3),
        scratch_shapes=[
            blk(bf16), blk(bf16), blk(bf16), blk(bf16), blk(bf16),
            pltpu.VMEM((RANK, CH), bf16), pltpu.VMEM((RANK, CH), bf16),
            pltpu.VMEM((2 * ROWS, 2 * ROWS), bf16), pltpu.VMEM((ROWS, 4 * ROWS), bf16),
            blk(bf16),
            blk(bf16),
            pltpu.VMEM((2, 128, 128), f32), pltpu.VMEM((128, 128), f32),
            pltpu.VMEM((XS, 128, 128), bf16), pltpu.VMEM((2, 128, 128), bf16),
            pltpu.VMEM((SEQ, ROWS, Q), bf16),
            pltpu.VMEM((SEQ - 1, ROWS, Q), bf16), pltpu.VMEM((SEQ, ROWS, Q), bf16),
            pltpu.VMEM((SEQ, 2 * ROWS, Q), f32), pltpu.VMEM((SEQ, 2 * ROWS, Q), f32),
            pltpu.VMEM((2 * ROWS, 2 * Q), bf16),
            pltpu.VMEM((SEQ, ROWS, Q), bf16),
            pltpu.VMEM((ZS, SL, CH), bf16), pltpu.VMEM((ZS, SL, CH), bf16),
            pltpu.VMEM((YS, SL, CH), bf16), pltpu.VMEM((SL, CH), bf16),
            dma((9,)), dma((2,)), dma((2,)), dma((XS,)), dma((XS,)),
            dma((SEQ,)), dma((SEQ,)), dma((SEQ,)), dma((SEQ,)), dma((SEQ,)), dma((SEQ,)),
            dma((ZS,)), dma((ZS,)), dma((YS,)), dma((YS,)), dma((ZS,)), dma((ZS,)), dma((3,)),
            pltpu.SemaphoreType.REGULAR,
        ],
        compiler_params=pltpu.CompilerParams(
            collective_id=0, has_side_effects=True, vmem_limit_bytes=60 * 1024 * 1024
        ),
        name="window_backward",
    )(
        second_gate_2[0], convolved_output[0], output_gradient[0], frozen_gradient[0], filt,
        adapter_down_weight.T, adapter_up_weight, tab, itab,
    )
    wide = jax.ShapeDtypeStruct((ROWS, CH), bf16)
    low = jax.ShapeDtypeStruct((RANK, CH), f32)
    grad_x1, grad_values, grad_x2, grad_a, grad_b = pl.pallas_call(
        results_kernel,
        out_shape=(wide, wide, wide, low, low),
        in_specs=[pl.BlockSpec(memory_space=pl.ANY)] * 5,
        out_specs=tuple([pl.BlockSpec(memory_space=pl.ANY)] * 5),
        scratch_shapes=[pltpu.VMEM((SEQ, ROWS, Q), bf16)] + [blk(bf16)] * 5
        + [pltpu.VMEM((ZS, SL, CH), bf16), pltpu.VMEM((2 * RANK, CH), f32), dma((8,)), dma((7,))],
        compiler_params=pltpu.CompilerParams(vmem_limit_bytes=60 * 1024 * 1024),
        name="results",
    )(mixed, grad_x2, slices, operator_values[0], first_gate_1[0])
    return grad_x1[None], grad_values[None], grad_x2[None], grad_a.T, grad_b


def solution(mesh):
    block = P("win", "seq", "chan")
    in_specs = (block,) * 6 + (P("seq", "chan"), P("chan", None), P(None, "chan"))
    out_specs = (block,) * 3 + (P("chan", None), P(None, "chan"))
    return jax.shard_map(
        on_device, mesh=mesh, in_specs=in_specs, out_specs=out_specs, check_vma=False
    )
```
